256 devices in a mesh: dp: 32 (over x, y, core), section: 8 (over z).
Axes of the slice: x: 4, y: 4, z: 8, core: 2. Of those that a mesh axis runs over, the one named last changes fastest.
Arguments:
- hidden_in: bfloat16 [8, 4096, 8192], P('section', 'dp'), may hold values from -6 to 6
- weight_rows: bfloat16 [8, 8192, 768], P('section', 'dp'), may hold values from -0.0625 to 0.0625
- x_in: bfloat16 [8, 4096, 12288], P('section', 'dp'), may hold values from -6 to 6
- c_in: bfloat16 [8, 4096, 768], P('section', 'dp'), may hold values from -0.59765625 to 0.59765625
- step_size: float32 [8, 4096, 192], P('section', 'dp'), may hold values from 0 to 1, as said below
- a_log: float32 [8, 192], P('section'), may hold values from 0.7 to 1.8
- out_grad: bfloat16 [8, 4096, 12288], P('section', 'dp'), may hold values from -6 to 6
Outputs:
- weight_grads: bfloat16 [8, 8192, 768], P('section', 'dp')
- next_cotangent: bfloat16 [8, 4096, 8192], P('section', 'dp')
- step_size_gradients: float32 [8, 4096, 192], P('section', 'dp')
The draws below stay inside these ranges and needn't reach their ends.
Inputs may be any that keep to these rules, and one draw needn't show every extreme that they name: `step_size`: positive step sizes.
All inputs are finite; a program needn't handle non-finite values.
Results may differ from the reference program's by a relative error of at most 0.025.
Values may be sent and summed in bfloat16 or wider, within the bound.
No kernel may reach another device: no remote copies, remote signals or barrier semaphores. Data moves between devices by JAX's collectives and lax.ppermute only.
A program may use at most 128 MiB of HBM per device.

```python
import jax
import jax.numpy as jnp
from jax import lax

D = 8192
HEADS = 192
HEAD_DIM = 64
STATE = 128
SPAN = 128
TOK_DEV = 128
SECTIONS = 8
TOKENS = 4096
GN = 768


def draw_step_size(key, part):
    key = jax.random.fold_in(key, 11)
    first, second, extra_factor_matrix, fourth = jax.random.split(key, 4)
    tensor_extent = (SECTIONS, TOKENS, HEADS)
    rough = jnp.exp(jax.random.uniform(first, tensor_extent, jnp.float32, -0.8, 0.8))
    share = 0.5
    quick = jax.random.uniform(fourth, (SECTIONS, 1, HEADS), jnp.float32) < share
    slow_step = 0.25 / TOK_DEV * rough
    fast_step = 0.015 * rough
    starting_position = jnp.where(quick, fast_step, slow_step)
    count = TOKENS // TOK_DEV
    places = jax.random.randint(second, (SECTIONS, count, 3), 0, TOK_DEV)
    within = jnp.arange(TOK_DEV)
    masked_positions = jnp.any(places[:, :, None, :] == within[None, None, :, None], axis=-1)
    masked_positions = masked_positions.reshape(SECTIONS, TOKENS)
    contiguous_span = jax.random.uniform(extra_factor_matrix, tensor_extent, jnp.float32, 0.06, 0.15)
    return jnp.where(masked_positions[:, :, None], contiguous_span, starting_position)


def raised(drawn, stream_key, source, target, blocks, factor):
    def block_of(dim):
        return (jnp.arange(drawn.shape[dim]) // (drawn.shape[dim] // blocks)).reshape((-1,) + (1,) * (drawn.ndim - 1 - dim))

    first = jax.random.permutation(stream_key, blocks)[block_of(target)]
    second = (block_of(target) + blocks // 2) % blocks
    return jnp.where((block_of(source) == first) | (block_of(source) == second), factor * drawn, drawn)


def levels(own_key, dims, cuts, least, largest):
    loudness = 1.0
    for axis_at, shards_of in cuts:
        heights = jax.random.uniform(jax.random.fold_in(jax.random.fold_in(own_key, 6), axis_at), (shards_of,), jnp.float32, least / len(cuts), largest / len(cuts))
        loudness = loudness * jnp.repeat(jnp.exp(heights), dims[axis_at] // shards_of).reshape((-1,) + (1,) * (len(dims) - 1 - axis_at))
    return loudness


def normal_values(stream_key, extent, deviation, bound, pieces=(), held_as=jnp.bfloat16):
    values = jax.random.normal(stream_key, extent, jnp.float32) * deviation
    if len(pieces) > 0:
        values = levels(stream_key, extent, pieces, -0.22, 0.18) * values
    return jnp.clip(values, min=-bound, max=bound).astype(held_as)


def bell_draw_with(rng, extent, deviation, reach, shards, heavy, held_as=jnp.bfloat16):
    values = deviation * jax.random.normal(rng, extent, jnp.float32)
    if shards:
        values = values * levels(rng, extent, shards, -0.22, 0.18)
    return jnp.clip(raised(values, jax.random.fold_in(rng, 3), *heavy), -reach, reach).astype(held_as)


def setup_inputs(seed: int = 0) -> dict:
    streams_of = jax.random.split(jax.random.key(seed), 8)
    return {
        "hidden_in": bell_draw_with(streams_of[0], (SECTIONS, TOKENS, D), 1.0, 6.0, ((0, 8), (1, 32)), (1, 2, 32, 2.75)),
        "weight_rows": normal_values(streams_of[1], (SECTIONS, D, GN), D ** -0.5, 0.0625, ((0, 8), (1, 32))),
        "x_in": normal_values(streams_of[2], (SECTIONS, TOKENS, HEADS * HEAD_DIM), 1.0, 6.0, ((0, 8), (1, 32))),
        "c_in": normal_values(streams_of[3], (SECTIONS, TOKENS, GN), 0.09, 0.59765625, ((0, 8), (1, 32))),
        "step_size": draw_step_size(jax.random.fold_in(streams_of[7], 71), 0),
        "a_log": jnp.clip(0.7 + 1.09999996 * jax.random.uniform(streams_of[5], (SECTIONS, HEADS), jnp.float32) ** levels(streams_of[5], (SECTIONS, HEADS), ((0, 8),), -0.2, 0.2), 0.7, 1.8),
        "out_grad": normal_values(streams_of[6], (SECTIONS, TOKENS, HEADS * HEAD_DIM), 1.0, 6.0, ((0, 8), (1, 32))),
    }


def scan_states(input_per_head, step_vals, rate, b_groups, c_groups):
    length = input_per_head.shape[0]
    blocks = length // SPAN
    heads = step_vals.shape[1]
    groups = b_groups.shape[1]
    per_group = heads // groups
    hp = lax.Precision.HIGHEST
    scaled = (input_per_head * step_vals[:, :, None]).reshape(blocks, SPAN, groups, per_group, -1)
    decay_logarithm = (-step_vals * rate[None, :]).reshape(blocks, SPAN, groups, per_group)
    cumul = jnp.cumsum(decay_logarithm, axis=1)
    b_blk = b_groups.reshape(blocks, SPAN, groups, -1)
    c_blk = c_groups.reshape(blocks, SPAN, groups, -1)
    scores = jnp.einsum('cign,cjgn->cgij', c_blk, b_blk, precision=hp)
    cumul_t = jnp.transpose(cumul, (0, 2, 3, 1))
    differ = cumul_t[..., :, None] - cumul_t[..., None, :]
    lower = jnp.arange(SPAN)[:, None] >= jnp.arange(SPAN)[None, :]
    decay = jnp.exp(jnp.where(lower, differ, -1e+30))
    weights = decay * scores[:, :, None]
    output_inside_block = jnp.einsum('cgkij,cjgkp->cigkp', weights, scaled, precision=hp)
    tail = jnp.exp(cumul[:, -1:] - cumul)
    states = jnp.einsum('cjgk,cjgkp,cjgn->cgkpn', tail, scaled, b_blk, precision=hp)
    totals = jnp.exp(cumul[:, -1])

    def carry_step(state_in, item):
        total_c, state_c = item
        return (total_c[:, :, None, None] * state_in + state_c, state_in)
    _, entering = lax.scan(carry_step, jnp.zeros(states.shape[1:], jnp.float32), (totals, states))
    y_inter = jnp.einsum('cign,cgkpn,cigk->cigkp', c_blk, entering, jnp.exp(cumul), precision=hp)
    return (output_inside_block + y_inter).reshape(length, heads, -1)

def backward_one(hidden_seq, weight_full, x_seq, c_seq, step_seq, rate, grad_seq):
    length = hidden_seq.shape[0]
    heads = step_seq.shape[1]
    groups = c_seq.shape[1] // STATE
    bproj = jnp.dot(hidden_seq, weight_full, preferred_element_type=jnp.float32).astype(jnp.bfloat16)
    input_per_head = x_seq.astype(jnp.float32).reshape(length, heads, -1)
    c_groups = c_seq.astype(jnp.float32).reshape(length, groups, STATE)
    cotan = grad_seq.astype(jnp.float32).reshape(length, heads, -1)

    def forward(bmat, steps):
        return scan_states(input_per_head, steps, rate, bmat.reshape(length, groups, STATE), c_groups)
    _, pullback_function = jax.vjp(forward, bproj.astype(jnp.float32), step_seq)
    grad_b32, step_grad = pullback_function(cotan)
    grad_b = grad_b32.astype(jnp.bfloat16)
    part16 = jnp.dot(hidden_seq.T, grad_b, preferred_element_type=jnp.float32).astype(jnp.bfloat16)
    partial_value = lax.optimization_barrier(part16).astype(jnp.float32)
    input_grad = jnp.dot(grad_b, weight_full.T, preferred_element_type=jnp.float32).astype(jnp.bfloat16)
    return (partial_value, input_grad, step_grad)

def reference(hidden_in, weight_rows, x_in, c_in, step_size, a_log, out_grad):
    count = TOKENS // TOK_DEV

    def section_work(items):
        hidden_s, weight_s, x_s, c_s, step_s, alog_s, grad_s = items
        rate = jnp.exp(alog_s)

        def seq_step(total, seq):
            hidden_q, x_q, c_q, step_q, grad_q = seq
            partial_value, input_grad, step_grad = backward_one(hidden_q, weight_s, x_q, c_q, step_q, rate, grad_q)
            return (total + partial_value, (input_grad, step_grad))
        seqs = (hidden_s.reshape(count, TOK_DEV, -1), x_s.reshape(count, TOK_DEV, -1), c_s.reshape(count, TOK_DEV, -1), step_s.reshape(count, TOK_DEV, -1), grad_s.reshape(count, TOK_DEV, -1))
        total, outs = lax.scan(seq_step, jnp.zeros(weight_s.shape, jnp.float32), seqs)
        inputs, steps_out = outs
        return (total.astype(jnp.bfloat16), inputs.reshape(TOKENS, -1), steps_out.reshape(TOKENS, -1))
    grads, inputs, step_size_gradients = lax.map(section_work, (hidden_in, weight_rows, x_in, c_in, step_size, a_log, out_grad))
    shifted = jnp.concatenate([inputs[1:], jnp.zeros_like(inputs[:1])], axis=0)
    return (grads, shifted, step_size_gradients)
```

```python
import functools

import jax
import jax.numpy as jnp
import numpy as np
from jax import lax
from jax.experimental import pallas as pl
from jax.experimental.pallas import tpu as pltpu
from jax.sharding import Mesh
from jax.sharding import PartitionSpec as P

STATE = 128
TOK = 128
HEADS = 192
GROUPS = 6
PER_GROUP = HEADS // GROUPS
HEAD_DIM = 64
RING = 4
HALF = 128
OFFSETS = (0, 3, 1, 2)
LOG2E = float(np.log2(np.e))
FAR_BELOW = -1e30
HP = lax.Precision.HIGHEST
F32 = jnp.float32
BF16 = jnp.bfloat16


def ring_shift(shard, axis, by):
    return lax.ppermute(shard, axis, [(i, (i + by) % RING) for i in range(RING)])


def swap_cores(shard):
    return lax.ppermute(shard, "core", [(0, 1), (1, 0)])


def to_previous_section(shard):
    return lax.ppermute(shard, "section", [(s, s - 1) for s in range(1, lax.axis_size("section"))])


def coordinates():
    return jnp.stack([lax.axis_index(a) for a in ("x", "y", "core")]).astype(jnp.int32)


def block_columns(where_ref, k, crossed):
    half, outer, inner = k // (RING * RING), k // RING % RING, k % RING
    dx, dy = (OFFSETS[inner], OFFSETS[outer]) if half == 0 else (OFFSETS[outer], OFFSETS[inner])
    chip = ((where_ref[0] + dx) % RING) * RING + (where_ref[1] + dy) % RING
    core = 1 - where_ref[2] if crossed else where_ref[2]
    return pl.multiple_of((chip * 2 + core) * 2 * HALF + half * HALF, HALF)


BLOCKS = 2 * RING * RING
VMEM_LIMIT = 16 * 2**20


def split_columns(where_ref, hidden, keep, send):
    for k in range(BLOCKS):
        to = slice(k * HALF, (k + 1) * HALF)
        keep[:, to] = hidden[:, pl.ds(block_columns(where_ref, k, False), HALF)]
        send[:, to] = hidden[:, pl.ds(block_columns(where_ref, k, True), HALF)]


def join_columns_kernel(orders, where_ref, *refs):
    pieces, out_ref = refs[:-1], refs[-1]
    for piece, order in zip(pieces, orders, strict=True):
        for j, k in enumerate(order):
            for side in range(2):
                columns = pl.ds(block_columns(where_ref, k, side == 1), HALF)
                out_ref[:, columns] = piece[side, :, j * HALF : (j + 1) * HALF]


def join_columns(where, pieces, orders, width):
    return pl.pallas_call(
        functools.partial(join_columns_kernel, orders),
        in_specs=[pl.BlockSpec(memory_space=pltpu.SMEM)]
        + [pl.BlockSpec(memory_space=pltpu.VMEM)] * len(pieces),
        out_specs=pl.BlockSpec(memory_space=pltpu.VMEM),
        out_shape=jax.ShapeDtypeStruct((TOK, width), BF16),
        cost_estimate=pl.CostEstimate(flops=0, bytes_accessed=4 * TOK * width, transcendentals=0),
        compiler_params=pltpu.CompilerParams(vmem_limit_bytes=VMEM_LIMIT),
        name="join_columns",
    )(where, *pieces)


def iotas():
    rows = lax.broadcasted_iota(jnp.int32, (TOK, TOK), 0)
    lanes = lax.broadcasted_iota(jnp.int32, (TOK, TOK), 1)
    return rows, lanes


def prepare(step_ref, alog_ref, rate_t, parts, left, right):
    rows, lanes = iotas()

    @pl.when(pl.program_id(0) == 0)
    def _():
        rate_t[...] = jnp.broadcast_to(jnp.exp(alog_ref[...]), (TOK, HEADS)).T
        left[:, :TOK] = (rows == lanes).astype(F32).astype(BF16)
        mask = jnp.where(rows >= lanes, 0.0, FAR_BELOW).astype(BF16)
        for h in range(PER_GROUP):
            at = slice(h * TOK, (h + 1) * TOK)
            chosen = (rows < 3 * PER_GROUP) & (rows % PER_GROUP == h)
            right[:TOK, at] = mask
            right[TOK:, at] = jnp.where(chosen, 1.0, 0.0).astype(BF16)

    upper = (rows <= lanes).astype(F32)
    rates = rate_t[group_rows(), :]
    cumul = jnp.dot(
        step_ref[...] * (rates * -LOG2E), upper, precision=HP, preferred_element_type=F32
    )
    high = cumul.astype(BF16).astype(F32)
    middle = (cumul - high).astype(BF16).astype(F32)
    low = cumul - high - middle
    ones = jnp.where(lax.broadcasted_iota(jnp.int32, (PER_GROUP, TOK), 0) < 3, 1.0, 0.0)
    left[:, TOK:] = jnp.concatenate([high, middle, low, ones], axis=0).T.astype(BF16)
    for i, part in enumerate((high, middle, low)):
        parts[i * PER_GROUP : (i + 1) * PER_GROUP, :] = part
    place = lax.broadcasted_iota(jnp.int32, (16, TOK), 0)
    for h in range(PER_GROUP):
        rest = jnp.zeros((16, TOK), F32)
        for i in range(3):
            rest = jnp.where(place == i, -parts[i * PER_GROUP + h : i * PER_GROUP + h + 1, :], rest)
        right[TOK + 3 * PER_GROUP : TOK + 3 * PER_GROUP + 16, h * TOK : (h + 1) * TOK] = rest.astype(BF16)
    return rates


def head_products(x_ref, grad_ref, step_ref, left, right):
    lanes = lax.broadcasted_iota(jnp.int32, (TOK, 2 * HEAD_DIM), 1)
    first = lanes < HEAD_DIM
    zero = jnp.zeros((), BF16)
    for pair in range(PER_GROUP // 2):
        at = slice(pair * 2 * HEAD_DIM, (pair + 1) * 2 * HEAD_DIM)
        both = x_ref[:, at]
        apart = jnp.concatenate([jnp.where(first, both, zero), jnp.where(first, zero, both)], axis=0)
        products = lax.dot_general(
            grad_ref[:, at], apart, (((1,), (1,)), ((), ())), preferred_element_type=F32
        )
        differ = jnp.dot(
            left[...], right[:, 2 * pair * TOK : 2 * (pair + 1) * TOK], preferred_element_type=F32
        )
        products = jnp.exp2(differ) * products
        for k in range(2):
            h = 2 * pair + k
            yield h, products[:, k * TOK : (k + 1) * TOK], step_ref[h : h + 1, :]


def group_rows():
    return pl.ds(pl.multiple_of(pl.program_id(0) * PER_GROUP, PER_GROUP), PER_GROUP)


def sum_of_heads(x_ref, grad_ref, c_ref, step_ref, left, right, out_ref):
    total = jnp.zeros((TOK, TOK), F32)
    for _, product, steps in head_products(x_ref, grad_ref, step_ref, left, right):
        total = total + product * steps
    grad_b = lax.dot_general(
        total, c_ref[...].astype(F32), (((0,), (0,)), ((), ())),
        precision=HP, preferred_element_type=F32,
    )
    out_ref[...] = grad_b.astype(BF16)


def grad_b_kernel(
    where_ref, x_ref, grad_ref, c_ref, step_ref, alog_ref, hidden_ref,
    out_ref, keep_ref, send_ref, rate_t, parts, left, right, hidden, keep, send, sem,
):
    g = pl.program_id(0)
    fetch = pltpu.make_async_copy(hidden_ref, hidden, sem.at[0])
    put_keep = pltpu.make_async_copy(keep, keep_ref, sem.at[1])
    put_send = pltpu.make_async_copy(send, send_ref, sem.at[2])

    @pl.when(g == 0)
    def _():
        fetch.start()

    prepare(step_ref, alog_ref, rate_t, parts, left, right)
    sum_of_heads(x_ref, grad_ref, c_ref, step_ref, left, right, out_ref)

    @pl.when(g == 1)
    def _():
        fetch.wait()
        split_columns(where_ref, hidden, keep, send)
        put_keep.start()
        put_send.start()

    @pl.when(g == GROUPS - 1)
    def _():
        put_keep.wait()
        put_send.wait()


def step_grad_kernel(
    x_ref, grad_ref, c_ref, b_ref, step_ref, alog_ref, out_ref, rate_t, parts, left, right, direct
):
    rates = prepare(step_ref, alog_ref, rate_t, parts, left, right)
    rows, lanes = iotas()
    scores = lax.dot_general(
        c_ref[...], b_ref[...], (((1,), (1,)), ((), ())), preferred_element_type=F32
    )
    by_row = jnp.zeros((TOK, TOK), F32)
    for h, product, steps in head_products(x_ref, grad_ref, step_ref, left, right):
        weighted = product * scores
        direct[h : h + 1, :] = jnp.sum(weighted, axis=0, keepdims=True)
        by_row = jnp.where(lanes == h, jnp.sum(weighted * steps, axis=1, keepdims=True), by_row)
    cumul_grad = by_row.T[:PER_GROUP] - direct[...] * step_ref[...]
    lower = (rows >= lanes).astype(F32)
    later = jnp.dot(cumul_grad, lower, precision=HP, preferred_element_type=F32)
    out_ref[...] = direct[...] - rates * later


WIDE = PER_GROUP * HEAD_DIM
BY_GROUP = pl.BlockSpec((TOK, STATE), lambda g: (0, g))
BY_HEADS = pl.BlockSpec((TOK, WIDE), lambda g: (0, g))
STEP_ROWS = pl.BlockSpec((PER_GROUP, TOK), lambda g: (g, 0))
WHOLE_RATE = pl.BlockSpec((1, HEADS), lambda g: (0, 0))
SCAN_SCRATCH = [
    pltpu.VMEM((HEADS, TOK), F32),
    pltpu.VMEM((3 * PER_GROUP, TOK), F32),
    pltpu.VMEM((TOK, 2 * TOK), BF16),
    pltpu.VMEM((2 * TOK, PER_GROUP * TOK), BF16),
]
SCAN_COST = pl.CostEstimate(
    flops=2 * HEADS * TOK * TOK * HEAD_DIM,
    bytes_accessed=4 * TOK * HEADS * HEAD_DIM,
    transcendentals=HEADS * TOK * TOK,
)


def scan_grad_b(where, x, grad, c, steps_t, a_log, hidden):
    anywhere = pl.BlockSpec(memory_space=pl.ANY)
    halved = jax.ShapeDtypeStruct((TOK, hidden.shape[1] // 2), hidden.dtype)
    return pl.pallas_call(
        grad_b_kernel,
        grid=(GROUPS,),
        in_specs=[
            pl.BlockSpec(memory_space=pltpu.SMEM),
            BY_HEADS, BY_HEADS, BY_GROUP, STEP_ROWS, WHOLE_RATE, anywhere,
        ],
        out_specs=[BY_GROUP, anywhere, anywhere],
        out_shape=[jax.ShapeDtypeStruct((TOK, GROUPS * STATE), BF16), halved, halved],
        scratch_shapes=SCAN_SCRATCH
        + [
            pltpu.VMEM(hidden.shape, BF16),
            pltpu.VMEM(halved.shape, BF16),
            pltpu.VMEM(halved.shape, BF16),
            pltpu.SemaphoreType.DMA((3,)),
        ],
        cost_estimate=SCAN_COST,
        compiler_params=pltpu.CompilerParams(vmem_limit_bytes=56 * 2**20),
        name="scan_grad_b",
    )(where, x, grad, c, steps_t, a_log, hidden)


def scan_step_grad(x, grad, c, b, steps_t, a_log):
    return pl.pallas_call(
        step_grad_kernel,
        grid=(GROUPS,),
        in_specs=[BY_HEADS, BY_HEADS, BY_GROUP, BY_GROUP, STEP_ROWS, WHOLE_RATE],
        out_specs=STEP_ROWS,
        out_shape=jax.ShapeDtypeStruct((HEADS, TOK), F32),
        scratch_shapes=SCAN_SCRATCH + [pltpu.VMEM((PER_GROUP, TOK), F32)],
        cost_estimate=SCAN_COST,
        compiler_params=pltpu.CompilerParams(vmem_limit_bytes=VMEM_LIMIT),
        name="scan_step_grad",
    )(x, grad, c, b, steps_t, a_log)


def rows_dot(a, b):
    return jnp.dot(a, b, preferred_element_type=F32)


def outer_dot(a, b):
    return lax.dot_general(a, b, (((0,), (0,)), ((), ())), preferred_element_type=F32)


def against_rows(a, w):
    return lax.dot_general(a, w, (((1,), (1,)), ((), ())), preferred_element_type=F32).astype(BF16)


def after(values, *done):
    return lax.optimization_barrier((values, done))[0]


def body(hidden_in, weight_rows, x_in, c_in, step_size, a_log, out_grad):
    hidden, weights = hidden_in[0], weight_rows[0]
    x, c, steps_t, grad = x_in[0], c_in[0], step_size[0].T, out_grad[0]
    where = coordinates()
    block = RING * HALF

    part_a, part_b = weights[:HALF], weights[HALF:]
    one_a = ring_shift(part_a, "x", 1), ring_shift(part_a, "x", -1)
    one_b = ring_shift(part_b, "y", 1), ring_shift(part_b, "y", -1)

    near_a = jnp.concatenate((part_a,) + one_a + (ring_shift(part_a, "x", 2),))
    near_b = jnp.concatenate((part_b,) + one_b + (ring_shift(part_b, "y", 2),))
    far_a = ring_shift(near_a, "y", 1), ring_shift(near_a, "y", -1)
    far_b = ring_shift(near_b, "x", 1), ring_shift(near_b, "x", -1)

    grad_b, kept, sent = scan_grad_b(after(where, near_a, near_b), x, grad, c, steps_t, a_log, hidden)
    other_b = swap_cores(grad_b)

    def pass_on(rows):
        own = against_rows(grad_b, rows)
        others = against_rows(other_b, rows)
        return to_previous_section(jnp.stack([own, swap_cores(others)]))

    passed = [pass_on(jnp.concatenate([near_a, near_b]))]

    half = block // 2
    other = swap_cores(sent)
    last_a = ring_shift(far_a[0][:half], "y", 1), ring_shift(far_a[1][half:], "y", -1)
    last_b = ring_shift(far_b[0][:half], "x", 1), ring_shift(far_b[1][half:], "x", -1)
    passed.append(pass_on(jnp.concatenate(far_a + far_b)))
    last_a, last_b = jnp.concatenate(last_a), jnp.concatenate(last_b)
    passed.append(pass_on(jnp.concatenate([last_a, last_b])))

    def payload(start, i):
        at = slice(start + i * block, start + (i + 1) * block)
        return jnp.concatenate([kept[:, at], other[:, at], grad_b], axis=1)

    start_b = RING * block
    sends_a, sends_b = after(
        ([payload(0, i) for i in (1, 2)], [payload(start_b, i) for i in (1, 2)]), last_a, last_b, passed[0]
    )
    arrived_a = [ring_shift(p, "y", by) for p, by in zip(sends_a, (-1, 1))]
    arrived_b = [ring_shift(p, "x", by) for p, by in zip(sends_b, (-1, 1))]
    send_a, send_b = after((payload(0, 3), payload(start_b, 3)), arrived_a, arrived_b)
    arrived_a.append(ring_shift(send_a, "y", 2))
    arrived_b.append(ring_shift(send_b, "x", 2))

    def partial_sums(start, arrived):
        at = slice(start, start + block)
        total = outer_dot(kept[:, at], grad_b) + outer_dot(other[:, at], other_b)
        for p in arrived:
            b = p[:, 2 * block :]
            total += outer_dot(p[:, :block], b) + outer_dot(p[:, block : 2 * block], swap_cores(b))
        return total

    def scattered(total, axis):
        parts = total.astype(BF16)
        result = total[:HALF]
        for i, by in ((1, -1), (2, 1), (3, 2)):
            result += ring_shift(parts[i * HALF : (i + 1) * HALF], axis, by).astype(F32)
        return result.astype(BF16)

    mine = jnp.zeros((TOK, GROUPS * STATE), F32)
    theirs = mine
    for start, rows in ((0, (near_a,) + far_a + (last_a,)), (start_b, (near_b,) + far_b + (last_b,))):
        for i, w in enumerate(rows):
            at = slice(start + i * block, start + (i + 1) * block)
            mine += rows_dot(kept[:, at], w)
            theirs += rows_dot(other[:, at], w)
    proj_b = (mine + swap_cores(theirs)).astype(BF16)
    step_grads_t = scan_step_grad(x, grad, c, proj_b, steps_t, a_log)

    sums_a, sums_b = after((partial_sums(0, arrived_a), partial_sums(start_b, arrived_b)), step_grads_t, passed[1])
    weight_grads = jnp.concatenate([scattered(sums_a, "x"), scattered(sums_b, "y")])

    each = RING * RING
    orders = (
        tuple(range(RING)) + tuple(range(each, each + RING)),
        tuple(range(RING, 3 * RING)) + tuple(range(each + RING, each + 3 * RING)),
        tuple(range(3 * RING, each)) + tuple(range(each + 3 * RING, 2 * each)),
    )
    joined = join_columns(where, passed, orders, hidden.shape[1])
    return weight_grads[None], joined[None], step_grads_t.T[None]


def solution(mesh):
    fine = Mesh(
        mesh.devices.reshape(RING, RING, 2, mesh.shape["section"]), ("x", "y", "core", "section")
    )
    dp = ("x", "y", "core")
    split = P("section", dp, None)
    in_specs = (split, split, split, split, split, P("section", None), split)
    return jax.shard_map(
        body, mesh=fine, in_specs=in_specs, out_specs=(split, split, split), check_vma=False
    )
```

```python
import functools

import jax
import jax.numpy as jnp
import numpy as np
from jax import lax
from jax.experimental import pallas as pl
from jax.experimental.pallas import tpu as pltpu
from jax.sharding import Mesh
from jax.sharding import PartitionSpec as P

STATE = 128
TOK = 128
HEADS = 192
GROUPS = 6
PER_GROUP = HEADS // GROUPS
HEAD_DIM = 64
RING = 4
SHARD = 256
OFFSETS = (0, 3, 1, 2)
LOG2E = float(np.log2(np.e))
FAR_BELOW = -1e30
HP = lax.Precision.HIGHEST
F32 = jnp.float32
BF16 = jnp.bfloat16


def ring_shift(shard, first, by):
    pairs = []
    for x in range(RING):
        for y in range(RING):
            for core in range(2):
                if first == (core == 0):
                    target = ((x + by) % RING, y)
                else:
                    target = (x, (y + by) % RING)
                pairs.append(((x * RING + y) * 2 + core, (target[0] * RING + target[1]) * 2 + core))
    return lax.ppermute(shard, ("x", "y", "core"), pairs)


def swap_cores(shard):
    return lax.ppermute(shard, "core", [(0, 1), (1, 0)])


def to_previous_section(shard):
    return lax.ppermute(shard, "section", [(s, s - 1) for s in range(1, lax.axis_size("section"))])


def coordinates():
    return jnp.stack([lax.axis_index(a) for a in ("x", "y", "core")]).astype(jnp.int32)


def block_columns(where_ref, k, crossed):
    core = 1 - where_ref[2] if crossed else where_ref[2]
    first, second = OFFSETS[k % RING], OFFSETS[k // RING]
    dx = first + core * (second - first)
    dy = second + core * (first - second)
    chip = ((where_ref[0] + dx) & (RING - 1)) * RING + ((where_ref[1] + dy) & (RING - 1))
    return pl.multiple_of((chip * 2 + core) * SHARD, SHARD)


BLOCKS = RING * RING
VMEM_LIMIT = 16 * 2**20
SMALL_COST = pl.CostEstimate(flops=0, bytes_accessed=1024, transcendentals=0)


def split_columns_kernel(where_ref, hidden_ref, keep_ref, send_ref):
    for k in range(BLOCKS):
        to = slice(k * SHARD, (k + 1) * SHARD)
        keep_ref[:, to] = hidden_ref[:, pl.ds(block_columns(where_ref, k, False), SHARD)]
        send_ref[:, to] = hidden_ref[:, pl.ds(block_columns(where_ref, k, True), SHARD)]


def split_columns(where, hidden):
    halved = jax.ShapeDtypeStruct((TOK, hidden.shape[1] // 2), hidden.dtype)
    in_vmem = pl.BlockSpec(memory_space=pltpu.VMEM)
    return pl.pallas_call(
        split_columns_kernel,
        in_specs=[pl.BlockSpec(memory_space=pltpu.SMEM), in_vmem],
        out_specs=[in_vmem, in_vmem],
        out_shape=[halved, halved],
        cost_estimate=SMALL_COST,
        compiler_params=pltpu.CompilerParams(vmem_limit_bytes=VMEM_LIMIT),
        name="split_columns",
    )(where, hidden)


def join_columns_kernel(orders, where_ref, *refs):
    pieces, out_ref = refs[:-1], refs[-1]
    for i, order in enumerate(orders):
        for side in range(2):
            for j, k in enumerate(order):
                columns = pl.ds(block_columns(where_ref, k, side == 1), SHARD)
                out_ref[:, columns] = pieces[2 * i + side][:TOK, j * SHARD : (j + 1) * SHARD]


def join_columns(where, pieces, orders, width):
    return pl.pallas_call(
        functools.partial(join_columns_kernel, orders),
        in_specs=[pl.BlockSpec(memory_space=pltpu.SMEM)]
        + [pl.BlockSpec(memory_space=pltpu.VMEM)] * len(pieces),
        out_specs=pl.BlockSpec(memory_space=pltpu.VMEM),
        out_shape=jax.ShapeDtypeStruct((TOK, width), BF16),
        cost_estimate=SMALL_COST,
        compiler_params=pltpu.CompilerParams(vmem_limit_bytes=VMEM_LIMIT),
        name="join_columns",
    )(where, *pieces)


def iotas():
    rows = lax.broadcasted_iota(jnp.int32, (TOK, TOK), 0)
    lanes = lax.broadcasted_iota(jnp.int32, (TOK, TOK), 1)
    return rows, lanes


def prepare(step_ref, alog_ref, rate_t, parts, left, right):
    rows, lanes = iotas()

    @pl.when(pl.program_id(0) == 0)
    def _():
        rate_t[...] = jnp.broadcast_to(jnp.exp(alog_ref[...]), (TOK, HEADS)).T
        left[:, :TOK] = (rows == lanes).astype(F32).astype(BF16)
        mask = jnp.where(rows >= lanes, 0.0, FAR_BELOW).astype(BF16)
        for h in range(PER_GROUP):
            at = slice(h * TOK, (h + 1) * TOK)
            chosen = (rows < 3 * PER_GROUP) & (rows % PER_GROUP == h)
            right[:TOK, at] = mask
            right[TOK:, at] = jnp.where(chosen, 1.0, 0.0).astype(BF16)

    upper = (rows <= lanes).astype(F32)
    rates = rate_t[group_rows(), :]
    cumul = jnp.dot(
        step_ref[...] * (rates * -LOG2E), upper, precision=HP, preferred_element_type=F32
    )
    high = cumul.astype(BF16).astype(F32)
    middle = (cumul - high).astype(BF16).astype(F32)
    low = cumul - high - middle
    ones = jnp.where(lax.broadcasted_iota(jnp.int32, (PER_GROUP, TOK), 0) < 3, 1.0, 0.0)
    left[:, TOK:] = jnp.concatenate([high, middle, low, ones], axis=0).T.astype(BF16)
    for i, part in enumerate((high, middle, low)):
        parts[i * PER_GROUP : (i + 1) * PER_GROUP, :] = part
    place = lax.broadcasted_iota(jnp.int32, (16, TOK), 0)
    for h in range(PER_GROUP):
        rest = jnp.zeros((16, TOK), F32)
        for i in range(3):
            rest = jnp.where(place == i, -parts[i * PER_GROUP + h : i * PER_GROUP + h + 1, :], rest)
        right[TOK + 3 * PER_GROUP : TOK + 3 * PER_GROUP + 16, h * TOK : (h + 1) * TOK] = rest.astype(BF16)
    return rates


def head_products(x_ref, grad_ref, step_ref, left, right):
    lanes = lax.broadcasted_iota(jnp.int32, (TOK, 2 * HEAD_DIM), 1)
    first = lanes < HEAD_DIM
    zero = jnp.zeros((), BF16)
    for pair in range(PER_GROUP // 2):
        at = slice(pair * 2 * HEAD_DIM, (pair + 1) * 2 * HEAD_DIM)
        both = x_ref[:, at]
        apart = jnp.concatenate([jnp.where(first, both, zero), jnp.where(first, zero, both)], axis=0)
        products = lax.dot_general(
            grad_ref[:, at], apart, (((1,), (1,)), ((), ())), preferred_element_type=F32
        )
        differ = jnp.dot(
            left[...], right[:, 2 * pair * TOK : 2 * (pair + 1) * TOK], preferred_element_type=F32
        )
        products = jnp.exp2(differ) * products
        for k in range(2):
            h = 2 * pair + k
            yield h, products[:, k * TOK : (k + 1) * TOK], step_ref[h : h + 1, :]


def group_rows():
    return pl.ds(pl.multiple_of(pl.program_id(0) * PER_GROUP, PER_GROUP), PER_GROUP)


def sum_of_heads(x_ref, grad_ref, c_ref, step_ref, left, right, out_ref):
    total = jnp.zeros((TOK, TOK), F32)
    for _, product, steps in head_products(x_ref, grad_ref, step_ref, left, right):
        total = total + product * steps
    grad_b = lax.dot_general(
        total, c_ref[...].astype(F32), (((0,), (0,)), ((), ())),
        precision=HP, preferred_element_type=F32,
    )
    out_ref[...] = grad_b.astype(BF16)


def grad_b_kernel(
    x_ref, grad_ref, c_ref, step_ref, alog_ref, out_ref, rate_t, parts, left, right
):
    prepare(step_ref, alog_ref, rate_t, parts, left, right)
    sum_of_heads(x_ref, grad_ref, c_ref, step_ref, left, right, out_ref)


def step_grad_kernel(
    x_ref, grad_ref, c_ref, b_ref, step_ref, alog_ref, out_ref, rate_t, parts, left, right, direct
):
    rates = prepare(step_ref, alog_ref, rate_t, parts, left, right)
    rows, lanes = iotas()
    scores = lax.dot_general(
        c_ref[...], b_ref[...], (((1,), (1,)), ((), ())), preferred_element_type=F32
    )
    by_row = jnp.zeros((TOK, TOK), F32)
    for h, product, steps in head_products(x_ref, grad_ref, step_ref, left, right):
        weighted = product * scores
        direct[h : h + 1, :] = jnp.sum(weighted, axis=0, keepdims=True)
        by_row = jnp.where(lanes == h, jnp.sum(weighted * steps, axis=1, keepdims=True), by_row)
    cumul_grad = by_row.T[:PER_GROUP] - direct[...] * step_ref[...]
    lower = (rows >= lanes).astype(F32)
    later = jnp.dot(cumul_grad, lower, precision=HP, preferred_element_type=F32)
    out_ref[...] = direct[...] - rates * later


WIDE = PER_GROUP * HEAD_DIM
BY_GROUP = pl.BlockSpec((TOK, STATE), lambda g: (0, g))
BY_HEADS = pl.BlockSpec((TOK, WIDE), lambda g: (0, g))
STEP_ROWS = pl.BlockSpec((PER_GROUP, TOK), lambda g: (g, 0))
WHOLE_RATE = pl.BlockSpec((1, HEADS), lambda g: (0, 0))
SCAN_SCRATCH = [
    pltpu.VMEM((HEADS, TOK), F32),
    pltpu.VMEM((3 * PER_GROUP, TOK), F32),
    pltpu.VMEM((TOK, 2 * TOK), BF16),
    pltpu.VMEM((2 * TOK, PER_GROUP * TOK), BF16),
]


def scan_grad_b(x, grad, c, steps_t, a_log):
    return pl.pallas_call(
        grad_b_kernel,
        grid=(GROUPS,),
        in_specs=[BY_HEADS, BY_HEADS, BY_GROUP, STEP_ROWS, WHOLE_RATE],
        out_specs=BY_GROUP,
        out_shape=jax.ShapeDtypeStruct((TOK, GROUPS * STATE), BF16),
        scratch_shapes=SCAN_SCRATCH,
        cost_estimate=SMALL_COST,
        compiler_params=pltpu.CompilerParams(vmem_limit_bytes=56 * 2**20),
        name="scan_grad_b",
    )(x, grad, c, steps_t, a_log)


def scan_step_grad(x, grad, c, b, steps_t, a_log):
    return pl.pallas_call(
        step_grad_kernel,
        grid=(GROUPS,),
        in_specs=[BY_HEADS, BY_HEADS, BY_GROUP, BY_GROUP, STEP_ROWS, WHOLE_RATE],
        out_specs=STEP_ROWS,
        out_shape=jax.ShapeDtypeStruct((HEADS, TOK), F32),
        scratch_shapes=SCAN_SCRATCH + [pltpu.VMEM((PER_GROUP, TOK), F32)],
        cost_estimate=SMALL_COST,
        compiler_params=pltpu.CompilerParams(vmem_limit_bytes=VMEM_LIMIT),
        name="scan_step_grad",
    )(x, grad, c, b, steps_t, a_log)


def rows_dot(a, b):
    return jnp.dot(a, b, preferred_element_type=F32)


def outer_dot(a, b):
    return lax.dot_general(a, b, (((0,), (0,)), ((), ())), preferred_element_type=F32)


def against_rows(a, w):
    return lax.dot_general(a, w, (((1,), (1,)), ((), ())), preferred_element_type=F32).astype(BF16)


def after(values, *done):
    return lax.optimization_barrier((values, done))[0]


def body(hidden_in, weight_rows, x_in, c_in, step_size, a_log, out_grad):
    hidden, part = hidden_in[0], weight_rows[0]
    x, c, steps_t, grad = x_in[0], c_in[0], step_size[0].T, out_grad[0]
    where = coordinates()
    block = RING * SHARD

    near = [ring_shift(part, True, by) for by in (1, -1, 2)]
    grad_b = scan_grad_b(x, grad, c, steps_t, a_log)
    near = jnp.concatenate([part] + after(near, grad_b))
    far = [ring_shift(near, False, by) for by in (1, -1)]
    both_b = jnp.concatenate([grad_b, swap_cores(grad_b)])

    def pass_on(rows, *done):
        both = after(to_previous_section(against_rows(both_b, rows)), *done)
        return both, swap_cores(both[TOK:])

    passed = [pass_on(near, far)]
    kept, sent = split_columns(after(where, both_b), hidden)
    both_hidden = jnp.concatenate([kept, swap_cores(sent)])

    half = block // 2
    last = jnp.concatenate([ring_shift(far[0][:half], False, 1), ring_shift(far[1][half:], False, -1)])

    def columns(i):
        return both_hidden[:, i * block : (i + 1) * block]

    def payload(i):
        return jnp.concatenate([columns(i), both_b], axis=1)

    sends = after([payload(1), payload(2)], far)
    arrived = [ring_shift(p, False, by) for p, by in zip(sends, (-1, 1))]
    arrived.append(ring_shift(after(payload(3), last, passed[0], arrived[0]), False, 2))

    proj = jnp.zeros((2 * TOK, GROUPS * STATE), F32)
    for i, rows in enumerate((near, *far, last)):
        proj += rows_dot(columns(i), rows)
    proj_b = (proj[:TOK] + swap_cores(proj[TOK:])).astype(BF16)
    step_grads_t = scan_step_grad(x, grad, c, proj_b, steps_t, a_log)

    arrived = [after(p, step_grads_t) for p in arrived]
    passed.append(pass_on(jnp.concatenate(far), step_grads_t))
    passed.append(pass_on(after(last, passed[1][0])))
    sums = outer_dot(columns(0), both_b)
    for p in arrived:
        sums += outer_dot(p[:, :block], p[:, block:])
    parts = after(sums.astype(BF16), passed[0], passed[1])
    shifts = ((1, -1), (2, 1), (3, 2))
    others = [ring_shift(parts[i * SHARD : (i + 1) * SHARD], True, by) for i, by in shifts]

    orders = (tuple(range(RING)), tuple(range(RING, 3 * RING)), tuple(range(3 * RING, 4 * RING)))
    joined = join_columns(where, passed[0] + passed[1] + passed[2], orders, hidden.shape[1])
    weight_grads = sums[:SHARD]
    for other in after(others, joined):
        weight_grads += other.astype(F32)
    return weight_grads.astype(BF16)[None], joined[None], step_grads_t.T[None]


def solution(mesh):
    fine = Mesh(
        mesh.devices.reshape(RING, RING, 2, mesh.shape["section"]), ("x", "y", "core", "section")
    )
    dp = ("x", "y", "core")
    split = P("section", dp, None)
    in_specs = (split, split, split, split, split, P("section", None), split)
    return jax.shard_map(
        body, mesh=fine, in_specs=in_specs, out_specs=(split, split, split), check_vma=False
    )
```

```python
import functools

import jax
import jax.numpy as jnp
import numpy as np
from jax import lax
from jax.experimental import pallas as pl
from jax.experimental.pallas import tpu as pltpu
from jax.sharding import Mesh
from jax.sharding import PartitionSpec as P

STATE = 128
TOK = 128
HEADS = 192
GROUPS = 6
PER_GROUP = HEADS // GROUPS
HEAD_DIM = 64
RING = 4
SHARD = 256
OFFSETS = (0, 3, 1, 2)
LOG2E = float(np.log2(np.e))
FAR_BELOW = -1e30
HP = lax.Precision.HIGHEST
F32 = jnp.float32
BF16 = jnp.bfloat16


def ring_shift(shard, first, by):
    pairs = []
    for x in range(RING):
        for y in range(RING):
            for core in range(2):
                if first == (core == 0):
                    target = ((x + by) % RING, y)
                else:
                    target = (x, (y + by) % RING)
                pairs.append(((x * RING + y) * 2 + core, (target[0] * RING + target[1]) * 2 + core))
    return lax.ppermute(shard, ("x", "y", "core"), pairs)


def swap_cores(shard):
    return lax.ppermute(shard, "core", [(0, 1), (1, 0)])


def to_previous_section(shard):
    return lax.ppermute(shard, "section", [(s, s - 1) for s in range(1, lax.axis_size("section"))])


def coordinates():
    return jnp.stack([lax.axis_index(a) for a in ("x", "y", "core")]).astype(jnp.int32)


def block_columns(where_ref, k, crossed):
    core = 1 - where_ref[2] if crossed else where_ref[2]
    first, second = OFFSETS[k % RING], OFFSETS[k // RING]
    dx = first + core * (second - first)
    dy = second + core * (first - second)
    chip = ((where_ref[0] + dx) & (RING - 1)) * RING + ((where_ref[1] + dy) & (RING - 1))
    return pl.multiple_of((chip * 2 + core) * SHARD, SHARD)


BLOCKS = RING * RING
VMEM_LIMIT = 16 * 2**20
SMALL_COST = pl.CostEstimate(flops=0, bytes_accessed=1024, transcendentals=0)


def split_columns_kernel(where_ref, hidden_ref, keep_ref, send_ref):
    for k in range(BLOCKS):
        to = slice(k * SHARD, (k + 1) * SHARD)
        keep_ref[:, to] = hidden_ref[:, pl.ds(block_columns(where_ref, k, False), SHARD)]
        send_ref[:, to] = hidden_ref[:, pl.ds(block_columns(where_ref, k, True), SHARD)]


def split_columns(where, hidden):
    halved = jax.ShapeDtypeStruct((TOK, hidden.shape[1] // 2), hidden.dtype)
    in_vmem = pl.BlockSpec(memory_space=pltpu.VMEM)
    return pl.pallas_call(
        split_columns_kernel,
        in_specs=[pl.BlockSpec(memory_space=pltpu.SMEM), in_vmem],
        out_specs=[in_vmem, in_vmem],
        out_shape=[halved, halved],
        cost_estimate=SMALL_COST,
        compiler_params=pltpu.CompilerParams(vmem_limit_bytes=VMEM_LIMIT),
        name="split_columns",
    )(where, hidden)


def join_columns_kernel(orders, where_ref, *refs):
    pieces, out_ref = refs[:-1], refs[-1]
    for i, order in enumerate(orders):
        for side in range(2):
            for j, k in enumerate(order):
                columns = pl.ds(block_columns(where_ref, k, side == 1), SHARD)
                out_ref[:, columns] = pieces[2 * i + side][:TOK, j * SHARD : (j + 1) * SHARD]


def join_columns(where, pieces, orders, width):
    return pl.pallas_call(
        functools.partial(join_columns_kernel, orders),
        in_specs=[pl.BlockSpec(memory_space=pltpu.SMEM)]
        + [pl.BlockSpec(memory_space=pltpu.VMEM)] * len(pieces),
        out_specs=pl.BlockSpec(memory_space=pltpu.VMEM),
        out_shape=jax.ShapeDtypeStruct((TOK, width), BF16),
        cost_estimate=SMALL_COST,
        compiler_params=pltpu.CompilerParams(vmem_limit_bytes=VMEM_LIMIT),
        name="join_columns",
    )(where, *pieces)


def iotas():
    rows = lax.broadcasted_iota(jnp.int32, (TOK, TOK), 0)
    lanes = lax.broadcasted_iota(jnp.int32, (TOK, TOK), 1)
    return rows, lanes


def prepare(step_ref, alog_ref, rate_t, parts, left, right, first=0):
    rows, lanes = iotas()

    @pl.when(pl.program_id(0) == 0)
    def _():
        rate_t[...] = jnp.broadcast_to(jnp.exp(alog_ref[...]), (TOK, HEADS)).T
        left[:, :TOK] = (rows == lanes).astype(F32).astype(BF16)
        mask = jnp.where(rows >= lanes, 0.0, FAR_BELOW).astype(BF16)
        for h in range(PER_GROUP):
            at = slice(h * TOK, (h + 1) * TOK)
            chosen = (rows < 3 * PER_GROUP) & (rows % PER_GROUP == h)
            right[:TOK, at] = mask
            right[TOK:, at] = jnp.where(chosen, 1.0, 0.0).astype(BF16)

    upper = (rows <= lanes).astype(F32)
    rates = rate_t[group_rows(first), :]
    cumul = jnp.dot(
        step_ref[...] * (rates * -LOG2E), upper, precision=HP, preferred_element_type=F32
    )
    high = cumul.astype(BF16).astype(F32)
    middle = (cumul - high).astype(BF16).astype(F32)
    low = cumul - high - middle
    ones = jnp.where(lax.broadcasted_iota(jnp.int32, (PER_GROUP, TOK), 0) < 3, 1.0, 0.0)
    left[:, TOK:] = jnp.concatenate([high, middle, low, ones], axis=0).T.astype(BF16)
    for i, part in enumerate((high, middle, low)):
        parts[i * PER_GROUP : (i + 1) * PER_GROUP, :] = part
    place = lax.broadcasted_iota(jnp.int32, (16, TOK), 0)
    for h in range(PER_GROUP):
        rest = jnp.zeros((16, TOK), F32)
        for i in range(3):
            rest = jnp.where(place == i, -parts[i * PER_GROUP + h : i * PER_GROUP + h + 1, :], rest)
        right[TOK + 3 * PER_GROUP : TOK + 3 * PER_GROUP + 16, h * TOK : (h + 1) * TOK] = rest.astype(BF16)
    return rates


def head_products(x_ref, grad_ref, step_ref, left, right):
    lanes = lax.broadcasted_iota(jnp.int32, (TOK, 2 * HEAD_DIM), 1)
    first = lanes < HEAD_DIM
    zero = jnp.zeros((), BF16)
    for pair in range(PER_GROUP // 2):
        at = slice(pair * 2 * HEAD_DIM, (pair + 1) * 2 * HEAD_DIM)
        both = x_ref[:, at]
        apart = jnp.concatenate([jnp.where(first, both, zero), jnp.where(first, zero, both)], axis=0)
        products = lax.dot_general(
            grad_ref[:, at], apart, (((1,), (1,)), ((), ())), preferred_element_type=F32
        )
        differ = jnp.dot(
            left[...], right[:, 2 * pair * TOK : 2 * (pair + 1) * TOK], preferred_element_type=F32
        )
        products = jnp.exp2(differ) * products
        for k in range(2):
            h = 2 * pair + k
            yield h, products[:, k * TOK : (k + 1) * TOK], step_ref[h : h + 1, :]


def group_rows(first):
    return pl.ds(pl.multiple_of((pl.program_id(0) + first) * PER_GROUP, PER_GROUP), PER_GROUP)


def sum_of_heads(x_ref, grad_ref, c_ref, step_ref, left, right, out_ref):
    total = jnp.zeros((TOK, TOK), F32)
    for _, product, steps in head_products(x_ref, grad_ref, step_ref, left, right):
        total = total + product * steps
    grad_b = lax.dot_general(
        total, c_ref[...].astype(F32), (((0,), (0,)), ((), ())),
        precision=HP, preferred_element_type=F32,
    )
    out_ref[...] = grad_b.astype(BF16)


def grad_b_kernel(
    x_ref, grad_ref, c_ref, step_ref, alog_ref, out_ref, rate_t, parts, left, right
):
    prepare(step_ref, alog_ref, rate_t, parts, left, right)
    sum_of_heads(x_ref, grad_ref, c_ref, step_ref, left, right, out_ref)


def step_grad_kernel(
    first, x_ref, grad_ref, c_ref, b_ref, step_ref, alog_ref, out_ref, rate_t, parts, left, right, direct
):
    rates = prepare(step_ref, alog_ref, rate_t, parts, left, right, first)
    rows, lanes = iotas()
    scores = lax.dot_general(
        c_ref[...], b_ref[...], (((1,), (1,)), ((), ())), preferred_element_type=F32
    )
    by_row = jnp.zeros((TOK, TOK), F32)
    for h, product, steps in head_products(x_ref, grad_ref, step_ref, left, right):
        weighted = product * scores
        direct[h : h + 1, :] = jnp.sum(weighted, axis=0, keepdims=True)
        by_row = jnp.where(lanes == h, jnp.sum(weighted * steps, axis=1, keepdims=True), by_row)
    cumul_grad = by_row.T[:PER_GROUP] - direct[...] * step_ref[...]
    lower = (rows >= lanes).astype(F32)
    later = jnp.dot(cumul_grad, lower, precision=HP, preferred_element_type=F32)
    out_ref[...] = direct[...] - rates * later


WIDE = PER_GROUP * HEAD_DIM
BY_GROUP = pl.BlockSpec((TOK, STATE), lambda g: (0, g))
BY_HEADS = pl.BlockSpec((TOK, WIDE), lambda g: (0, g))
STEP_ROWS = pl.BlockSpec((PER_GROUP, TOK), lambda g: (g, 0))
WHOLE_RATE = pl.BlockSpec((1, HEADS), lambda g: (0, 0))
SCAN_SCRATCH = [
    pltpu.VMEM((HEADS, TOK), F32),
    pltpu.VMEM((3 * PER_GROUP, TOK), F32),
    pltpu.VMEM((TOK, 2 * TOK), BF16),
    pltpu.VMEM((2 * TOK, PER_GROUP * TOK), BF16),
]


def scan_grad_b(x, grad, c, steps_t, a_log):
    return pl.pallas_call(
        grad_b_kernel,
        grid=(GROUPS,),
        in_specs=[BY_HEADS, BY_HEADS, BY_GROUP, STEP_ROWS, WHOLE_RATE],
        out_specs=BY_GROUP,
        out_shape=jax.ShapeDtypeStruct((TOK, GROUPS * STATE), BF16),
        scratch_shapes=SCAN_SCRATCH,
        cost_estimate=SMALL_COST,
        compiler_params=pltpu.CompilerParams(vmem_limit_bytes=56 * 2**20),
        name="scan_grad_b",
    )(x, grad, c, steps_t, a_log)


def scan_step_grad(x, grad, c, b, steps_t, a_log, first, count):
    by_heads = pl.BlockSpec((TOK, WIDE), lambda g: (0, g + first))
    by_group = pl.BlockSpec((TOK, STATE), lambda g: (0, g + first))
    return pl.pallas_call(
        functools.partial(step_grad_kernel, first),
        grid=(count,),
        in_specs=[
            by_heads, by_heads, by_group, by_group,
            pl.BlockSpec((PER_GROUP, TOK), lambda g: (g + first, 0)), WHOLE_RATE,
        ],
        out_specs=STEP_ROWS,
        out_shape=jax.ShapeDtypeStruct((count * PER_GROUP, TOK), F32),
        scratch_shapes=SCAN_SCRATCH + [pltpu.VMEM((PER_GROUP, TOK), F32)],
        cost_estimate=SMALL_COST,
        compiler_params=pltpu.CompilerParams(vmem_limit_bytes=VMEM_LIMIT),
        name="scan_step_grad",
    )(x, grad, c, b, steps_t, a_log)


def rows_dot(a, b):
    return jnp.dot(a, b, preferred_element_type=F32)


def outer_dot(a, b):
    return lax.dot_general(a, b, (((0,), (0,)), ((), ())), preferred_element_type=F32)


def against_rows(a, w):
    return lax.dot_general(a, w, (((1,), (1,)), ((), ())), preferred_element_type=F32).astype(BF16)


def after(values, *done):
    return lax.optimization_barrier((values, done))[0]


def body(hidden_in, weight_rows, x_in, c_in, step_size, a_log, out_grad):
    hidden, part = hidden_in[0], weight_rows[0]
    x, c, steps_t, grad = x_in[0], c_in[0], step_size[0].T, out_grad[0]
    where = coordinates()
    block = RING * SHARD

    near = [ring_shift(part, True, by) for by in (1, -1, 2)]
    grad_b = scan_grad_b(x, grad, c, steps_t, a_log)
    near = jnp.concatenate([part] + after(near, grad_b))
    far = [ring_shift(near, False, by) for by in (1, -1)]
    other_b = swap_cores(grad_b)
    both_b = jnp.concatenate([grad_b, other_b])

    def pass_on(rows):
        return to_previous_section(against_rows(both_b, rows))

    def both_columns(both):
        return both, swap_cores(both[TOK:])

    near_passed = pass_on(near)
    kept, sent = split_columns(where, hidden)
    passed = [both_columns(after(near_passed, far))]
    both_hidden = jnp.concatenate([kept, swap_cores(sent)])

    half = block // 2
    last = jnp.concatenate([ring_shift(far[0][:half], False, 1), ring_shift(far[1][half:], False, -1)])

    def columns(i):
        return both_hidden[:, i * block : (i + 1) * block]

    def payload(i):
        return jnp.concatenate([columns(i), both_b], axis=1)

    sends = after([payload(1), payload(2)], far, passed[0][0])
    arrived = [ring_shift(p, False, by) for p, by in zip(sends, (-1, 1))]
    arrived.append(ring_shift(after(payload(3), last, arrived), False, 2))

    proj = jnp.zeros((2 * TOK, GROUPS * STATE), F32)
    for i, rows in enumerate((near, *far, last)):
        proj += rows_dot(columns(i), rows)
    proj_b = (proj[:TOK] + swap_cores(proj[TOK:])).astype(BF16)
    cut = GROUPS // 2
    early_grads = scan_step_grad(x, grad, c, proj_b, steps_t, a_log, 0, cut)
    passed.append(both_columns(after(pass_on(jnp.concatenate(far)), early_grads)))
    last_passed = pass_on(after(last, passed[1][0]))
    arrived = [after(p, early_grads) for p in arrived]
    sums = outer_dot(columns(0), both_b)
    for p in arrived:
        sums += outer_dot(p[:, :block], p[:, block:])
    parts = after(sums.astype(BF16), passed[0], passed[1])
    shifts = ((1, -1), (2, 1), (3, 2))
    others = [ring_shift(parts[i * SHARD : (i + 1) * SHARD], True, by) for i, by in shifts]

    late_b = after(proj_b, parts)
    late_grads = scan_step_grad(x, grad, c, late_b, steps_t, a_log, cut, GROUPS - cut)
    step_grads_t = jnp.concatenate([early_grads, late_grads])
    passed.append(both_columns(after(last_passed, late_grads)))

    orders = (tuple(range(RING)), tuple(range(RING, 3 * RING)), tuple(range(3 * RING, 4 * RING)))
    joined = join_columns(where, passed[0] + passed[1] + passed[2], orders, hidden.shape[1])
    weight_grads = sums[:SHARD]
    for other in after(others, joined, step_grads_t):
        weight_grads += other.astype(F32)
    return weight_grads.astype(BF16)[None], joined[None], step_grads_t.T[None]


def solution(mesh):
    fine = Mesh(
        mesh.devices.reshape(RING, RING, 2, mesh.shape["section"]), ("x", "y", "core", "section")
    )
    dp = ("x", "y", "core")
    split = P("section", dp, None)
    in_specs = (split, split, split, split, split, P("section", None), split)
    return jax.shard_map(
        body, mesh=fine, in_specs=in_specs, out_specs=(split, split, split), check_vma=False
    )
```

```python
import functools

import jax
import jax.numpy as jnp
import numpy as np
from jax import lax
from jax.experimental import pallas as pl
from jax.experimental.pallas import tpu as pltpu
from jax.sharding import Mesh
from jax.sharding import PartitionSpec as P

STATE = 128
TOK = 128
HEADS = 192
GROUPS = 6
PER_GROUP = HEADS // GROUPS
HEAD_DIM = 64
RING = 4
SHARD = 256
OFFSETS = (0, 3, 1, 2)
LOG2E = float(np.log2(np.e))
FAR_BELOW = -1e30
HP = lax.Precision.HIGHEST
F32 = jnp.float32
BF16 = jnp.bfloat16


def ring_shift(shard, first, by):
    pairs = []
    for x in range(RING):
        for y in range(RING):
            for core in range(2):
                if first == (core == 0):
                    target = ((x + by) % RING, y)
                else:
                    target = (x, (y + by) % RING)
                pairs.append(((x * RING + y) * 2 + core, (target[0] * RING + target[1]) * 2 + core))
    return lax.ppermute(shard, ("x", "y", "core"), pairs)


def swap_cores(shard):
    return lax.ppermute(shard, "core", [(0, 1), (1, 0)])


def to_previous_section(shard):
    return lax.ppermute(shard, "section", [(s, s - 1) for s in range(1, lax.axis_size("section"))])


def coordinates():
    return jnp.stack([lax.axis_index(a) for a in ("x", "y", "core")]).astype(jnp.int32)


def block_columns(where_ref, k, crossed):
    core = 1 - where_ref[2] if crossed else where_ref[2]
    first, second = OFFSETS[k % RING], OFFSETS[k // RING]
    dx = first + core * (second - first)
    dy = second + core * (first - second)
    chip = ((where_ref[0] + dx) & (RING - 1)) * RING + ((where_ref[1] + dy) & (RING - 1))
    return pl.multiple_of((chip * 2 + core) * SHARD, SHARD)


BLOCKS = RING * RING
VMEM_LIMIT = 16 * 2**20
SMALL_COST = pl.CostEstimate(flops=0, bytes_accessed=1024, transcendentals=0)


def split_columns_kernel(where_ref, hidden_ref, keep_ref, send_ref):
    for k in range(BLOCKS):
        to = slice(k * SHARD, (k + 1) * SHARD)
        keep_ref[:, to] = hidden_ref[:, pl.ds(block_columns(where_ref, k, False), SHARD)]
        send_ref[:, to] = hidden_ref[:, pl.ds(block_columns(where_ref, k, True), SHARD)]


def split_columns(where, hidden):
    halved = jax.ShapeDtypeStruct((TOK, hidden.shape[1] // 2), hidden.dtype)
    in_vmem = pl.BlockSpec(memory_space=pltpu.VMEM)
    return pl.pallas_call(
        split_columns_kernel,
        in_specs=[pl.BlockSpec(memory_space=pltpu.SMEM), in_vmem],
        out_specs=[in_vmem, in_vmem],
        out_shape=[halved, halved],
        cost_estimate=SMALL_COST,
        compiler_params=pltpu.CompilerParams(vmem_limit_bytes=VMEM_LIMIT),
        name="split_columns",
    )(where, hidden)


def join_columns_kernel(orders, where_ref, *refs):
    pieces, out_ref = refs[:-1], refs[-1]
    for i, order in enumerate(orders):
        for side in range(2):
            for j, k in enumerate(order):
                columns = pl.ds(block_columns(where_ref, k, side == 1), SHARD)
                out_ref[:, columns] = pieces[2 * i + side][:TOK, j * SHARD : (j + 1) * SHARD]


def join_columns(where, pieces, orders, width):
    return pl.pallas_call(
        functools.partial(join_columns_kernel, orders),
        in_specs=[pl.BlockSpec(memory_space=pltpu.SMEM)]
        + [pl.BlockSpec(memory_space=pltpu.VMEM)] * len(pieces),
        out_specs=pl.BlockSpec(memory_space=pltpu.VMEM),
        out_shape=jax.ShapeDtypeStruct((TOK, width), BF16),
        cost_estimate=SMALL_COST,
        compiler_params=pltpu.CompilerParams(vmem_limit_bytes=VMEM_LIMIT),
        name="join_columns",
    )(where, *pieces)


def iotas():
    rows = lax.broadcasted_iota(jnp.int32, (TOK, TOK), 0)
    lanes = lax.broadcasted_iota(jnp.int32, (TOK, TOK), 1)
    return rows, lanes


def prepare(step_ref, alog_ref, rate_t, parts, left, right, first=0):
    rows, lanes = iotas()

    @pl.when(pl.program_id(0) == 0)
    def _():
        rate_t[...] = jnp.broadcast_to(jnp.exp(alog_ref[...]), (TOK, HEADS)).T
        left[:, :TOK] = (rows == lanes).astype(F32).astype(BF16)
        mask = jnp.where(rows >= lanes, 0.0, FAR_BELOW).astype(BF16)
        for h in range(PER_GROUP):
            at = slice(h * TOK, (h + 1) * TOK)
            chosen = (rows < 3 * PER_GROUP) & (rows % PER_GROUP == h)
            right[:TOK, at] = mask
            right[TOK:, at] = jnp.where(chosen, 1.0, 0.0).astype(BF16)

    upper = (rows <= lanes).astype(F32)
    rates = rate_t[group_rows(first), :]
    cumul = jnp.dot(
        step_ref[...] * (rates * -LOG2E), upper, precision=HP, preferred_element_type=F32
    )
    high = cumul.astype(BF16).astype(F32)
    middle = (cumul - high).astype(BF16).astype(F32)
    low = cumul - high - middle
    ones = jnp.where(lax.broadcasted_iota(jnp.int32, (PER_GROUP, TOK), 0) < 3, 1.0, 0.0)
    left[:, TOK:] = jnp.concatenate([high, middle, low, ones], axis=0).T.astype(BF16)
    for i, part in enumerate((high, middle, low)):
        parts[i * PER_GROUP : (i + 1) * PER_GROUP, :] = part
    place = lax.broadcasted_iota(jnp.int32, (16, TOK), 0)
    for h in range(PER_GROUP):
        rest = jnp.zeros((16, TOK), F32)
        for i in range(3):
            rest = jnp.where(place == i, -parts[i * PER_GROUP + h : i * PER_GROUP + h + 1, :], rest)
        right[TOK + 3 * PER_GROUP : TOK + 3 * PER_GROUP + 16, h * TOK : (h + 1) * TOK] = rest.astype(BF16)
    return rates


def head_products(x_ref, grad_ref, step_ref, left, right):
    lanes = lax.broadcasted_iota(jnp.int32, (TOK, 2 * HEAD_DIM), 1)
    first = lanes < HEAD_DIM
    zero = jnp.zeros((), BF16)
    for pair in range(PER_GROUP // 2):
        at = slice(pair * 2 * HEAD_DIM, (pair + 1) * 2 * HEAD_DIM)
        both = x_ref[:, at]
        apart = jnp.concatenate([jnp.where(first, both, zero), jnp.where(first, zero, both)], axis=0)
        products = lax.dot_general(
            grad_ref[:, at], apart, (((1,), (1,)), ((), ())), preferred_element_type=F32
        )
        differ = jnp.dot(
            left[...], right[:, 2 * pair * TOK : 2 * (pair + 1) * TOK], preferred_element_type=F32
        )
        products = jnp.exp2(differ) * products
        for k in range(2):
            h = 2 * pair + k
            yield h, products[:, k * TOK : (k + 1) * TOK], step_ref[h : h + 1, :]


def group_rows(first):
    return pl.ds(pl.multiple_of((pl.program_id(0) + first) * PER_GROUP, PER_GROUP), PER_GROUP)


def sum_of_heads(x_ref, grad_ref, c_ref, step_ref, left, right, out_ref):
    total = jnp.zeros((TOK, TOK), F32)
    for _, product, steps in head_products(x_ref, grad_ref, step_ref, left, right):
        total = total + product * steps
    grad_b = lax.dot_general(
        total, c_ref[...].astype(F32), (((0,), (0,)), ((), ())),
        precision=HP, preferred_element_type=F32,
    )
    out_ref[...] = grad_b.astype(BF16)


def grad_b_kernel(
    x_ref, grad_ref, c_ref, step_ref, alog_ref, out_ref, rate_t, parts, left, right
):
    prepare(step_ref, alog_ref, rate_t, parts, left, right)
    sum_of_heads(x_ref, grad_ref, c_ref, step_ref, left, right, out_ref)


def step_grad_kernel(
    first, x_ref, grad_ref, c_ref, b_ref, step_ref, alog_ref, out_ref, rate_t, parts, left, right, direct
):
    rates = prepare(step_ref, alog_ref, rate_t, parts, left, right, first)
    rows, lanes = iotas()
    scores = lax.dot_general(
        c_ref[...], b_ref[...], (((1,), (1,)), ((), ())), preferred_element_type=F32
    )
    by_row = jnp.zeros((TOK, TOK), F32)
    for h, product, steps in head_products(x_ref, grad_ref, step_ref, left, right):
        weighted = product * scores
        direct[h : h + 1, :] = jnp.sum(weighted, axis=0, keepdims=True)
        by_row = jnp.where(lanes == h, jnp.sum(weighted * steps, axis=1, keepdims=True), by_row)
    cumul_grad = by_row.T[:PER_GROUP] - direct[...] * step_ref[...]
    lower = (rows >= lanes).astype(F32)
    later = jnp.dot(cumul_grad, lower, precision=HP, preferred_element_type=F32)
    out_ref[...] = direct[...] - rates * later


WIDE = PER_GROUP * HEAD_DIM
BY_GROUP = pl.BlockSpec((TOK, STATE), lambda g: (0, g))
BY_HEADS = pl.BlockSpec((TOK, WIDE), lambda g: (0, g))
STEP_ROWS = pl.BlockSpec((PER_GROUP, TOK), lambda g: (g, 0))
WHOLE_RATE = pl.BlockSpec((1, HEADS), lambda g: (0, 0))
SCAN_SCRATCH = [
    pltpu.VMEM((HEADS, TOK), F32),
    pltpu.VMEM((3 * PER_GROUP, TOK), F32),
    pltpu.VMEM((TOK, 2 * TOK), BF16),
    pltpu.VMEM((2 * TOK, PER_GROUP * TOK), BF16),
]


def scan_grad_b(x, grad, c, steps_t, a_log):
    return pl.pallas_call(
        grad_b_kernel,
        grid=(GROUPS,),
        in_specs=[BY_HEADS, BY_HEADS, BY_GROUP, STEP_ROWS, WHOLE_RATE],
        out_specs=BY_GROUP,
        out_shape=jax.ShapeDtypeStruct((TOK, GROUPS * STATE), BF16),
        scratch_shapes=SCAN_SCRATCH,
        cost_estimate=SMALL_COST,
        compiler_params=pltpu.CompilerParams(vmem_limit_bytes=56 * 2**20),
        name="scan_grad_b",
    )(x, grad, c, steps_t, a_log)


def scan_step_grad(x, grad, c, b, steps_t, a_log, first, count):
    by_heads = pl.BlockSpec((TOK, WIDE), lambda g: (0, g + first))
    by_group = pl.BlockSpec((TOK, STATE), lambda g: (0, g + first))
    return pl.pallas_call(
        functools.partial(step_grad_kernel, first),
        grid=(count,),
        in_specs=[
            by_heads, by_heads, by_group, by_group,
            pl.BlockSpec((PER_GROUP, TOK), lambda g: (g + first, 0)), WHOLE_RATE,
        ],
        out_specs=STEP_ROWS,
        out_shape=jax.ShapeDtypeStruct((count * PER_GROUP, TOK), F32),
        scratch_shapes=SCAN_SCRATCH + [pltpu.VMEM((PER_GROUP, TOK), F32)],
        cost_estimate=SMALL_COST,
        compiler_params=pltpu.CompilerParams(vmem_limit_bytes=VMEM_LIMIT),
        name="scan_step_grad",
    )(x, grad, c, b, steps_t, a_log)


def rows_dot(a, b):
    return jnp.dot(a, b, preferred_element_type=F32)


def outer_dot(a, b):
    return lax.dot_general(a, b, (((0,), (0,)), ((), ())), preferred_element_type=F32)


def against_rows(a, w):
    return lax.dot_general(a, w, (((1,), (1,)), ((), ())), preferred_element_type=F32).astype(BF16)


def after(values, *done):
    return lax.optimization_barrier((values, done))[0]


def body(hidden_in, weight_rows, x_in, c_in, step_size, a_log, out_grad):
    hidden, part = hidden_in[0], weight_rows[0]
    x, c, steps_t, grad = x_in[0], c_in[0], step_size[0].T, out_grad[0]
    where = coordinates()
    block = RING * SHARD

    near = [ring_shift(part, True, by) for by in (1, -1, 2)]
    grad_b = scan_grad_b(x, grad, c, steps_t, a_log)
    near = jnp.concatenate([part] + after(near, grad_b))
    following = ring_shift(near, False, -1)
    far = [ring_shift(near, False, 1), following]
    other_b = swap_cores(grad_b)
    both_b = jnp.concatenate([grad_b, other_b])

    def pass_on(rows):
        return to_previous_section(against_rows(both_b, rows))

    def both_columns(both):
        return both, swap_cores(both[TOK:])

    near_passed = pass_on(near)
    kept, sent = split_columns(where, hidden)
    passed = [both_columns(after(near_passed, far))]
    both_hidden = jnp.concatenate([kept, swap_cores(sent)])

    half = block // 2
    upper = ring_shift(far[1][half:], False, -1)
    last = jnp.concatenate([ring_shift(far[0][:half], False, 1), upper])

    def columns(i):
        return both_hidden[:, i * block : (i + 1) * block]

    def payload(i):
        return jnp.concatenate([columns(i), both_b], axis=1)

    sends = after([payload(1), payload(2)], far, passed[0][0])
    arrived = [ring_shift(p, False, by) for p, by in zip(sends, (-1, 1))]
    arrived.append(ring_shift(after(payload(3), last, arrived), False, 2))

    proj = jnp.zeros((2 * TOK, GROUPS * STATE), F32)
    for i, rows in enumerate((near, *far, last)):
        proj += rows_dot(columns(i), rows)
    proj_b = (proj[:TOK] + swap_cores(proj[TOK:])).astype(BF16)
    cut = GROUPS // 2
    early_grads = scan_step_grad(x, grad, c, proj_b, steps_t, a_log, 0, cut)
    passed.append(both_columns(after(pass_on(jnp.concatenate(far)), early_grads)))
    last_passed = pass_on(after(last, passed[1][0]))
    arrived = [after(p, early_grads) for p in arrived]
    sums = outer_dot(columns(0), both_b)
    for p in arrived:
        sums += outer_dot(p[:, :block], p[:, block:])
    parts = after(sums.astype(BF16), passed[0], passed[1])
    shifts = ((1, -1), (2, 1), (3, 2))
    others = [ring_shift(parts[i * SHARD : (i + 1) * SHARD], True, by) for i, by in shifts]

    late_b = after(proj_b, parts)
    late_grads = scan_step_grad(x, grad, c, late_b, steps_t, a_log, cut, GROUPS - cut)
    step_grads_t = jnp.concatenate([early_grads, late_grads])
    passed.append(both_columns(after(last_passed, late_grads)))

    orders = (tuple(range(RING)), tuple(range(RING, 3 * RING)), tuple(range(3 * RING, 4 * RING)))
    joined = join_columns(where, passed[0] + passed[1] + passed[2], orders, hidden.shape[1])
    weight_grads = sums[:SHARD]
    for other in after(others, joined, step_grads_t):
        weight_grads += other.astype(F32)
    return weight_grads.astype(BF16)[None], joined[None], step_grads_t.T[None]


def solution(mesh):
    fine = Mesh(
        mesh.devices.reshape(RING, RING, 2, mesh.shape["section"]), ("x", "y", "core", "section")
    )
    dp = ("x", "y", "core")
    split = P("section", dp, None)
    in_specs = (split, split, split, split, split, P("section", None), split)
    return jax.shard_map(
        body, mesh=fine, in_specs=in_specs, out_specs=(split, split, split), check_vma=False
    )
```
